32 devices in a mesh: section: 2 (over x), grp: 16 (over z, y, core).
Axes of the slice: x: 2, y: 2, z: 4, core: 2. Of those that a mesh axis runs over, the one named last changes fastest.
Arguments:
- voltages: bfloat16 [1024, 524288], P('grp', 'section'), may hold values from -6 to 6
- filter_taps: float32 [8, 512], replicated, may hold values from -2 to 2
- beam_weights: bfloat16 [256, 2, 512, 1024], P('grp'), may hold values from -0.125 to 0.125
- antenna_of_row: int32 [1024], replicated, may hold values from 0 to 1023, each once
- beam_delay: int32 [512], P('grp'), may hold values from 0 to 127
Outputs:
- dedispersed: float32 [256, 2, 512, 1024], P(None, None, 'grp', 'section')
The draws below stay inside these ranges and needn't reach their ends.
Inputs may be any that keep to these rules, and one draw needn't show every extreme that they name: A permutation: voltage row r holds physical antenna antenna_of_row[r].
All inputs are finite; a program needn't handle non-finite values.
Results may differ from the reference program's by a relative error of at most 0.0069.
Values may be sent and summed in bfloat16 or wider, within the bound.
No kernel may reach another device: no remote copies, remote signals or barrier semaphores. Data moves between devices by JAX's collectives and lax.ppermute only.
A program may use at most 320 MiB of HBM per device.

```python
import math
import jax
import jax.numpy as jnp
from jax import lax

ANTENNAS = 1024
FRAME = 512
CHANNELS = 256
TAPS = 8
BEAMS = 512
DFT_LEN = 256
ADVANCE = 128
SPECTRA = 1024
SAMPLES = 524288


def plant(values, rng, low, high):
    dims = values.shape
    spot = [jax.random.randint(jax.random.fold_in(rng, axis), (), 0, dims[axis]) for axis in range(len(dims))]
    values = values.at[tuple(spot)].set(low)
    longest = dims.index(max(dims))
    spot[longest] = (spot[longest] + 1) % dims[longest]
    return values.at[tuple(spot)].set(high)


def shard_levels(own_key, dims, split, least, largest):
    level = 1.0
    for position, parts in split:
        steps = jax.random.uniform(jax.random.fold_in(jax.random.fold_in(own_key, 6), position), (parts,), jnp.float32, least / len(split), largest / len(split))
        level = level * jnp.repeat(jnp.exp(steps), dims[position] // parts).reshape((-1,) + (1,) * (len(dims) - 1 - position))
    return level


def gaussian(stream_key, extent, spread, bound, pieces=(), kind=jnp.bfloat16):
    values = jax.random.normal(stream_key, extent, jnp.float32) * spread
    if len(pieces) > 0:
        values = shard_levels(stream_key, extent, pieces, -0.22, 0.18) * values
    return jnp.clip(values, min=-bound, max=bound).astype(kind)


def setup_inputs(seed: int = 0) -> dict:
    key_of = jax.random.split(jax.random.key(seed), 6)
    voltages = gaussian(key_of[0], (ANTENNAS, SAMPLES), 1.0, 6.0, ((0, 16), (1, 2)))
    filter_taps = gaussian(key_of[1], (TAPS, FRAME), TAPS ** -0.5, 2.0, (), jnp.float32)
    beam_weights = gaussian(key_of[2], (CHANNELS, 2, BEAMS, ANTENNAS), (2 * ANTENNAS) ** -0.5, 0.125, ((0, 16),))
    antenna_of_row = jax.random.permutation(key_of[3], ANTENNAS).astype(jnp.int32)
    beam_delay = plant(jax.random.randint(key_of[4], (BEAMS,), 0, DFT_LEN // 2), jax.random.fold_in(key_of[4], 1), 0, (DFT_LEN // 2) - 1).astype(jnp.int32)
    return dict(voltages=voltages, filter_taps=filter_taps, beam_weights=beam_weights, antenna_of_row=antenna_of_row, beam_delay=beam_delay)


def rounded(values):
    return lax.optimization_barrier(values.astype(jnp.bfloat16))


def channel_table(frame_length):
    channels = frame_length // 2
    column = jnp.arange(frame_length, dtype=jnp.int32)
    channel = column % channels
    quadrature = column // channels
    sample = jnp.arange(frame_length, dtype=jnp.int32)[:, None]
    winding = (sample * channel[None, :]) % frame_length
    angles = (2.0 * math.pi / frame_length) * winding.astype(jnp.float32)
    factor = channels ** -0.5
    dft_cols = jnp.where(quadrature[None, :] == 0, jnp.cos(angles) * factor, -jnp.sin(angles) * factor)
    return dft_cols.astype(jnp.bfloat16)


def block_tables(length):
    half_len = length // 2
    factor = length ** -0.5
    sample = jnp.arange(length, dtype=jnp.int32)
    angles = (2.0 * math.pi / length) * ((sample[:, None] * sample[None, :]) % length).astype(jnp.float32)
    cosine_table = (jnp.cos(angles) * factor).astype(jnp.bfloat16)
    sine_table = (jnp.sin(angles) * factor).astype(jnp.bfloat16)
    forward_real = jnp.concatenate([cosine_table, -sine_table], axis=1)
    forward_imag = jnp.concatenate([sine_table, cosine_table], axis=1)
    back_cos = cosine_table[:, half_len:]
    back_sin = sine_table[:, half_len:]
    inverse_real = jnp.concatenate([back_cos, back_sin], axis=1)
    inverse_imag = jnp.concatenate([-back_sin, back_cos], axis=1)
    return forward_real, forward_imag, inverse_real, inverse_imag


def chirp_factor(delays, channel_start, channel_count, channels, length):
    frequency = jnp.arange(length, dtype=jnp.int32)
    signed = jnp.where(frequency < length // 2, frequency, frequency - length).astype(jnp.float32)
    channel = (channel_start + jnp.arange(channel_count, dtype=jnp.int32)).astype(jnp.float32)
    strength = (1.0 + channel / channels) ** -3.0
    sweep = signed * signed / (length * length)
    phases = (math.pi * delays.astype(jnp.float32))[None, :, None] * strength[:, None, None] * sweep[None, None, :] - (0.5 * math.pi) * frequency.astype(jnp.float32)[None, None, :]
    return jnp.cos(phases), jnp.sin(phases)


def channelise(antenna_block, filter_taps, dft_cols):
    row_count = antenna_block.shape[0]
    past_samples = jnp.zeros((row_count, (TAPS - 1) * FRAME), jnp.bfloat16)
    extended = jnp.concatenate([past_samples, antenna_block], axis=1).reshape(row_count, SPECTRA + TAPS - 1, FRAME)
    weighted = jnp.zeros((row_count, SPECTRA, FRAME), jnp.float32)
    for tap_index in range(TAPS):
        weighted = weighted + filter_taps[tap_index] * extended[:, tap_index:tap_index + SPECTRA, :].astype(jnp.float32)
    weighted = rounded(weighted)
    product = jnp.einsum("asp,pj->ajs", weighted.astype(jnp.float32), dft_cols.astype(jnp.float32), precision=lax.Precision.HIGHEST)
    return rounded(product)


def reference(voltages, filter_taps, beam_weights, antenna_of_row, beam_delay):
    dft_cols = channel_table(FRAME)
    block_rows = math.gcd(ANTENNAS, 64)
    grouped = voltages.reshape(ANTENNAS // block_rows, block_rows, SAMPLES)
    channelised = lax.map(lambda antenna_block: channelise(antenna_block, filter_taps, dft_cols), grouped)
    channelised = channelised.reshape(ANTENNAS, FRAME, SPECTRA)
    by_column = jnp.moveaxis(channelised, 1, 0)

    def form_channel(inputs):
        steering_weights, part_real, part_imag = inputs
        ordered = jnp.take(steering_weights, antenna_of_row, axis=2).astype(jnp.float32)
        real_in = part_real.astype(jnp.float32)
        imag_in = part_imag.astype(jnp.float32)
        beam_real = jnp.dot(ordered[0], real_in, precision=lax.Precision.HIGHEST) - jnp.dot(ordered[1], imag_in, precision=lax.Precision.HIGHEST)
        beam_imag = jnp.dot(ordered[0], imag_in, precision=lax.Precision.HIGHEST) + jnp.dot(ordered[1], real_in, precision=lax.Precision.HIGHEST)
        return rounded(jnp.stack([beam_real, beam_imag]))

    beamed = lax.map(form_channel, (beam_weights, by_column[:CHANNELS], by_column[CHANNELS:]))
    forward_real, forward_imag, inverse_real, inverse_imag = [table_part.astype(jnp.float32) for table_part in block_tables(DFT_LEN)]

    def dedisperse_channel(inputs):
        series, channel = inputs
        block_count = SPECTRA // ADVANCE
        leading = jnp.zeros((2, BEAMS, ADVANCE), jnp.bfloat16)
        joined = jnp.concatenate([leading, series], axis=2).reshape(2, BEAMS, block_count + 1, ADVANCE)
        blocks = jnp.concatenate([joined[:, :, :-1, :], joined[:, :, 1:, :]], axis=3).astype(jnp.float32)
        spectrum = jnp.einsum("bml,lk->bmk", blocks[0], forward_real, precision=lax.Precision.HIGHEST) + jnp.einsum("bml,lk->bmk", blocks[1], forward_imag, precision=lax.Precision.HIGHEST)
        chirp_real, chirp_imag = chirp_factor(beam_delay, channel, 1, CHANNELS, DFT_LEN)
        chirp_real = chirp_real[0][:, None, :]
        chirp_imag = chirp_imag[0][:, None, :]
        spec_real = spectrum[:, :, :DFT_LEN]
        spec_imag = spectrum[:, :, DFT_LEN:]
        filtered_real = rounded(spec_real * chirp_real - spec_imag * chirp_imag).astype(jnp.float32)
        filtered_imag = rounded(spec_real * chirp_imag + spec_imag * chirp_real).astype(jnp.float32)
        result = jnp.einsum("bmk,kn->bmn", filtered_real, inverse_real, precision=lax.Precision.HIGHEST) + jnp.einsum("bmk,kn->bmn", filtered_imag, inverse_imag, precision=lax.Precision.HIGHEST)
        out_real = result[:, :, :ADVANCE].reshape(BEAMS, SPECTRA)
        out_imag = result[:, :, ADVANCE:].reshape(BEAMS, SPECTRA)
        return jnp.stack([out_real, out_imag])

    return lax.map(dedisperse_channel, (beamed, jnp.arange(CHANNELS, dtype=jnp.int32)))
```

```python
import functools
import math

import jax
import jax.numpy as jnp
import numpy as np
from jax import lax
from jax.experimental import pallas as pl
from jax.experimental.pallas import tpu as pltpu
from jax.sharding import PartitionSpec as P

DFT_LEN = 256
GAP = 8
ANTENNA_BLOCK = 16
VMEM_LIMIT = 56 * 1024 * 1024


def shifted(value, axis, steps):
    count = lax.axis_size(axis)
    leading, last = (max(0, -steps), min(count, count - steps))
    return lax.ppermute(value, axis, [(source, source + steps) for source in range(leading, last)])


def dft_rows(frame_length, group_count):
    channels = frame_length // 2
    per_target = channels // group_count
    row = np.arange(frame_length)
    target = row // (2 * per_target)
    within = row % (2 * per_target)
    quadrature = within // per_target
    channel = target * per_target + within % per_target
    winding = np.arange(frame_length)[None, :] * channel[:, None] % frame_length
    angles = np.float32(2.0 * math.pi / frame_length) * winding.astype(np.float32)
    factor = np.float32(channels ** (-0.5))
    table = np.where(quadrature[:, None] == 0, np.cos(angles) * factor, -np.sin(angles) * factor)
    return jnp.asarray(table.astype(jnp.bfloat16))


def block_tables(length):
    half_len = length // 2
    factor = length ** (-0.5)
    sample = jnp.arange(length, dtype=jnp.int32)
    angles = (
        2.0 * math.pi / length * (sample[:, None] * sample[None, :] % length).astype(jnp.float32)
    )
    cosine_table = (jnp.cos(angles) * factor).astype(jnp.bfloat16)
    sine_table = (jnp.sin(angles) * factor).astype(jnp.bfloat16)
    forward_real = jnp.concatenate([cosine_table, -sine_table], axis=1)
    forward_imag = jnp.concatenate([sine_table, cosine_table], axis=1)
    back_cos = cosine_table[:, half_len:]
    back_sin = sine_table[:, half_len:]
    inverse_real = jnp.concatenate([back_cos, back_sin], axis=1)
    inverse_imag = jnp.concatenate([-back_sin, back_cos], axis=1)
    return (forward_real, forward_imag, inverse_real, inverse_imag)


def chirp_factor(delays, channel_count, channels, length):
    frequency = jnp.arange(length, dtype=jnp.int32)
    signed = jnp.where(frequency < length // 2, frequency, frequency - length).astype(jnp.float32)
    channel = jnp.arange(channel_count, dtype=jnp.int32).astype(jnp.float32)
    strength = (1.0 + channel / channels) ** (-3.0)
    sweep = signed * signed / (length * length)
    phases = (math.pi * delays.astype(jnp.float32))[None, :, None] * strength[
        :, None, None
    ] * sweep[None, None, :] - 0.5 * math.pi * frequency.astype(jnp.float32)[None, None, :]
    return (jnp.cos(phases), jnp.sin(phases))


def channelise_kernel(taps, frame, spectra, edge, *refs):
    taps_ref, table_ref, past_ref, now_ref = refs[:4]
    out_ref, w_ref, x_ref = refs[-3:]
    rows = now_ref.shape[0]
    past_frames = past_ref.shape[1] // frame
    group = 8
    lanes = 128
    at_edge = pl.program_id(0) == 0

    def filter_group(frames, first, lane):
        weights = [
            jnp.broadcast_to(taps_ref[k : k + 1, lane : lane + lanes], (8, lanes))
            for k in range(taps)
        ]
        for half in range(rows // 8):
            part = [f[half * 8 : half * 8 + 8] for f in frames]
            for i in range(group):
                total = weights[0] * part[i]
                for k in range(1, taps):
                    total = total + weights[k] * part[i + k]
                at = pl.multiple_of((first + i) * (rows + GAP) + half * 8, 8)
                w_ref[lane // lanes, pl.ds(at, 8), :] = total

    def earlier(start):
        value = past_ref[:, start : start + lanes]
        if edge:
            value = jnp.where(at_edge, refs[4][:, start : start + lanes], value)
        return value

    for lane in range(0, frame, lanes):
        frames = []
        for i in range(1 - taps, group):
            if i < 0:
                value = earlier((i + past_frames) * frame + lane)
            else:
                value = now_ref[:, i * frame + lane : i * frame + lane + lanes]
            frames.append(value.astype(jnp.float32))
        filter_group(frames, 0, lane)

    def later(step, carry):
        for lane in range(0, frame, lanes):
            frames = []
            for i in range(1 - taps, group):
                start = pl.multiple_of((step * group + i) * frame + lane, lanes)
                frames.append(now_ref[:, pl.ds(start, lanes)].astype(jnp.float32))
            filter_group(frames, step * group, lane)
        return carry

    lax.fori_loop(1, spectra // group, later, 0)

    def transform(pair, carry):
        parts = []
        for i in range(2):
            row = [
                w_ref[lane, pl.ds(pair * 2 + i, spectra, stride=rows + GAP), :].astype(jnp.bfloat16)
                for lane in range(frame // lanes)
            ]
            parts.append(jnp.concatenate(row, axis=1))
        both = jnp.concatenate(parts, axis=0)
        result = lax.dot_general(
            table_ref[...], both, (((1,), (1,)), ((), ())), preferred_element_type=jnp.float32
        )
        for i in range(2):
            at = pl.multiple_of((pair * 2 + i) * (frame + GAP), GAP)
            x_ref[pl.ds(at, frame), :] = result[:, i * spectra : (i + 1) * spectra]
        return carry

    lax.fori_loop(0, rows // 2, transform, 0, unroll=4)

    def arrange(step, carry):
        for i in range(8):
            j = step * 8 + i
            out_ref[j] = x_ref[pl.ds(j, rows, stride=frame + GAP), :].astype(jnp.bfloat16)
        return carry

    lax.fori_loop(0, frame // 8, arrange, 0)


def channelise(voltages, halo, filter_taps, table, first, count, spectra, low, high):
    taps, frame = filter_taps.shape
    rows = ANTENNA_BLOCK
    past_frames = halo.shape[1] // frame
    per_block = spectra // past_frames
    base = low // rows
    edge = first == 0
    operands = [filter_taps, table, voltages, voltages]
    specs = [
        pl.BlockSpec((taps, frame), lambda t, a: (0, 0)),
        pl.BlockSpec((frame, frame), lambda t, a: (0, 0)),
        pl.BlockSpec(
            (rows, past_frames * frame),
            lambda t, a: (base + a, jnp.maximum((first + t) * per_block - 1, 0)),
        ),
        pl.BlockSpec((rows, spectra * frame), lambda t, a: (base + a, first + t)),
    ]
    if edge:
        operands.append(halo)
        specs.append(pl.BlockSpec((rows, past_frames * frame), lambda t, a: (base + a, 0)))
    return pl.pallas_call(
        functools.partial(channelise_kernel, taps, frame, spectra, edge),
        grid=(count, (high - low) // rows),
        in_specs=specs,
        out_specs=pl.BlockSpec((frame, rows, spectra), lambda t, a: (0, a, t)),
        out_shape=jax.ShapeDtypeStruct((frame, high - low, count * spectra), jnp.bfloat16),
        scratch_shapes=[
            pltpu.VMEM((frame // 128, (spectra + 1) * (rows + GAP), 128), jnp.float32),
            pltpu.VMEM(((rows + 1) * (frame + GAP), spectra), jnp.float32),
        ],
        compiler_params=pltpu.CompilerParams(vmem_limit_bytes=VMEM_LIMIT),
        cost_estimate=pl.CostEstimate(
            flops=4 * count * (high - low) * spectra * frame * frame,
            bytes_accessed=4 * count * (high - low) * spectra * frame,
            transcendentals=0,
        ),
        name="channelise",
    )(*operands)


def beamform_kernel(cuts, weights_ref, *refs):
    out_ref = refs[-1]
    inputs = refs[:-1]
    groups = out_ref.shape[0]
    spectra = out_ref.shape[-1]
    beams = weights_ref.shape[2]

    def rows_of(quadrature):
        parts = []
        for ref in inputs[quadrature::2]:
            bounds = [0] + (cuts if len(inputs) == 2 else []) + [ref.shape[2]]
            for low, high in zip(bounds[:-1], bounds[1:]):
                parts.append(ref[:, 0, low:high, :].reshape(groups * (high - low), spectra))
        return parts[0] if len(parts) == 1 else jnp.concatenate(parts, axis=0)

    both = jnp.concatenate([rows_of(0), rows_of(1)], axis=1)
    share = beams // groups
    step = max(share, 128)
    for first in range(0, beams, step):
        by_real = jnp.dot(
            weights_ref[0, 0, first : first + step], both, preferred_element_type=jnp.float32
        )
        by_imag = jnp.dot(
            weights_ref[0, 1, first : first + step], both, preferred_element_type=jnp.float32
        )
        beam_real = (by_real[:, :spectra] - by_imag[:, spectra:]).astype(jnp.bfloat16)
        beam_imag = (by_real[:, spectra:] + by_imag[:, :spectra]).astype(jnp.bfloat16)
        low = first // share
        high = low + step // share
        out_ref[low:high, 0, 0] = beam_real.reshape(step // share, share, spectra)
        out_ref[low:high, 0, 1] = beam_imag.reshape(step // share, share, spectra)


def beamform(weights, received, cuts, first, count, spectra, low, high):
    per_target, _, beams, antennas = weights.shape
    groups = received[0].shape[0]
    share = beams // groups
    specs = [pl.BlockSpec((1, 2, beams, antennas), lambda c, t: (low + c, 0, 0, 0))]
    operands = [weights]
    for array in received:
        block = (groups, 1, array.shape[2], spectra)
        specs.append(pl.BlockSpec(block, lambda c, t: (0, low + c, 0, first + t)))
        specs.append(pl.BlockSpec(block, lambda c, t: (0, per_target + low + c, 0, first + t)))
        operands += [array, array]
    return pl.pallas_call(
        functools.partial(beamform_kernel, cuts),
        grid=(high - low, count),
        in_specs=specs,
        out_specs=pl.BlockSpec((groups, 1, 2, share, spectra), lambda c, t: (0, c, 0, 0, t)),
        out_shape=jax.ShapeDtypeStruct(
            (groups, high - low, 2, share, count * spectra), jnp.bfloat16
        ),
        compiler_params=pltpu.CompilerParams(vmem_limit_bytes=VMEM_LIMIT),
        cost_estimate=pl.CostEstimate(
            flops=8 * (high - low) * beams * antennas * spectra * count,
            bytes_accessed=4 * (high - low) * beams * (antennas + 2 * spectra * count),
            transcendentals=0,
        ),
        name="beamform",
    )(*operands)


def dedisperse_kernel(count, *refs):
    pieces = refs[: count + 1]
    cos_ref, sin_ref, fr_ref, fi_ref, ir_ref, ii_ref = refs[count + 1 : count + 7]
    out_ref = refs[-1]
    sources, chans, _, beams, advance = pieces[0].shape
    length = 2 * advance
    merged = sources * chans * beams
    chirp_real = cos_ref[...].reshape(merged, length)
    chirp_imag = sin_ref[...].reshape(merged, length)

    def part(ref, quadrature):
        return ref[:, :, quadrature].reshape(merged, advance)

    for m in range(count):
        before, after = pieces[m], pieces[m + 1]
        real = jnp.concatenate([part(before, 0), part(after, 0)], axis=1)
        imag = jnp.concatenate([part(before, 1), part(after, 1)], axis=1)
        spectrum = jnp.dot(real, fr_ref[...], preferred_element_type=jnp.float32) + jnp.dot(
            imag, fi_ref[...], preferred_element_type=jnp.float32
        )
        spec_real = spectrum[:, :length]
        spec_imag = spectrum[:, length:]
        filtered_real = (spec_real * chirp_real - spec_imag * chirp_imag).astype(jnp.bfloat16)
        filtered_imag = (spec_real * chirp_imag + spec_imag * chirp_real).astype(jnp.bfloat16)
        result = jnp.dot(filtered_real, ir_ref[...], preferred_element_type=jnp.float32) + jnp.dot(
            filtered_imag, ii_ref[...], preferred_element_type=jnp.float32
        )
        at = slice(m * advance, (m + 1) * advance)
        out_ref[:, :, 0, :, at] = result[:, :advance].reshape(sources, chans, beams, advance)
        out_ref[:, :, 1, :, at] = result[:, advance:].reshape(sources, chans, beams, advance)


def dedisperse(pieces, first, blocks, low, high, chans, chirp, tables, output):
    count = len(pieces) - 1
    groups, per_target, beams, length = chirp[0].shape
    advance = length // 2
    sources = max(1, min(groups, 1024 // (beams * chans)))

    def piece_spec(block, start):
        skip = (low - start) // chans
        return pl.BlockSpec(
            (sources, chans, 2, beams, advance), lambda g, c: (g, skip + c, 0, 0, block)
        )

    base = low // chans
    factor = pl.BlockSpec((sources, chans, beams, length), lambda g, c: (g, base + c, 0, 0))
    specs = [piece_spec(block, start) for _, block, start in pieces] + [factor] * 2
    specs += [pl.BlockSpec(t.shape, lambda g, c: (0, 0)) for t in tables]
    operands = [array for array, _, _ in pieces] + list(chirp) + list(tables)
    aliases = {}
    if output is not None:
        aliases = {len(operands): 0}
        operands.append(output)
        specs.append(pl.BlockSpec(memory_space=pl.ANY))
    return pl.pallas_call(
        functools.partial(dedisperse_kernel, count),
        grid=(groups // sources, (high - low) // chans),
        in_specs=specs,
        out_specs=pl.BlockSpec(
            (sources, chans, 2, beams, count * advance),
            lambda g, c: (g, base + c, 0, 0, first // count),
        ),
        out_shape=jax.ShapeDtypeStruct(
            (groups, per_target, 2, beams, blocks * advance), jnp.float32
        ),
        input_output_aliases=aliases,
        compiler_params=pltpu.CompilerParams(vmem_limit_bytes=VMEM_LIMIT),
        cost_estimate=pl.CostEstimate(
            flops=12 * count * groups * (high - low) * beams * length * length,
            bytes_accessed=groups * (high - low) * beams * advance * (12 * count + 20),
            transcendentals=0,
        ),
        name="dedisperse",
    )(*operands)


def local(voltages, filter_taps, beam_weights, antenna_of_row, beam_delay):
    group_count = lax.axis_size("grp")
    antenna_rows, samples = voltages.shape
    taps, frame = filter_taps.shape
    spectra = samples // frame
    channels = frame // 2
    antennas = antenna_of_row.shape[0]
    per_target = channels // group_count
    advance = DFT_LEN // 2
    blocks = spectra // advance
    last = blocks - 1

    table = dft_rows(frame, group_count)
    past_frames = -(-(taps - 1) // 8) * 8
    halo = shifted(voltages[:, samples - past_frames * frame :], "section", 1)

    cut = ANTENNA_BLOCK
    cuts = [cut] if cut < antenna_rows else []
    bounds = [0] + cuts + [antenna_rows]
    row_order = np.concatenate(
        [
            (np.arange(group_count)[:, None] * antenna_rows + np.arange(low, high)[None, :]).ravel()
            for low, high in zip(bounds[:-1], bounds[1:])
        ]
    )
    chosen = (
        jnp.arange(antennas, dtype=jnp.int32)[:, None] == antenna_of_row[row_order][None, :]
    ).astype(jnp.bfloat16)
    ordered = jnp.einsum(
        "ckba,ar->ckbr", beam_weights, chosen, preferred_element_type=jnp.float32
    ).astype(jnp.bfloat16)
    tables = block_tables(DFT_LEN)
    chirp = chirp_factor(beam_delay, channels, channels, DFT_LEN)
    chirp = tuple(c.reshape((group_count, per_target) + c.shape[1:]) for c in chirp)

    previous = None

    def exchange(value, previous):
        if previous is not None:
            value, previous = lax.optimization_barrier((value, previous))
        return lax.all_to_all(value, "grp", split_axis=0, concat_axis=0, tiled=True)

    def send_spectra(first, count, low, high, previous):
        value = channelise(voltages, halo, filter_taps, table, first, count, advance, low, high)
        value = value.reshape(group_count, 2 * per_target, high - low, count * advance)
        return exchange(value, previous)

    received_last = []
    for low, high in zip(bounds[:-1], bounds[1:]):
        previous = send_spectra(last, 1, low, high, previous)
        received_last.append(previous)
    received_rest = previous = send_spectra(0, last, 0, antenna_rows, previous)

    form = functools.partial(beamform, ordered)
    whole = (0, per_target)
    value = form(received_last, cuts, 0, 1, advance, *whole)
    value, chirp = lax.optimization_barrier((value, chirp))
    series_last = previous = exchange(value, previous)
    leading = shifted(series_last, "section", 1)
    value = form([received_rest], cuts, 0, last - 1, advance, *whole)
    series_early = previous = exchange(value, previous)

    tail = max(1, per_target // 4)
    middle = per_target - tail
    value = form([received_rest], cuts, last - 1, 1, advance, 0, middle)
    value, leading = lax.optimization_barrier((value, leading))
    series_head = previous = exchange(value, previous)
    value = form([received_rest], cuts, last - 1, 1, advance, middle, per_target)
    early = [(leading, 0, 0)] + [(series_early, m, 0) for m in range(last - 1)]
    output = dedisperse(early, 0, blocks, 0, per_target, tail, chirp, tables, None)
    value, output = lax.optimization_barrier((value, output))
    series_tail = exchange(value, previous)

    before, after = (series_early, last - 2, 0), (series_last, 0, 0)
    for low, high, series in ((0, middle, series_head), (middle, per_target, series_tail)):
        pieces = [before, (series, 0, low), after]
        output = dedisperse(pieces, last - 1, blocks, low, high, tail, chirp, tables, output)
    return output.reshape((channels,) + output.shape[2:])


def solution(mesh):
    in_specs = (P("grp", "section"), P(), P("grp", None, None, None), P(), P("grp"))
    out_specs = P(None, None, "grp", "section")
    return jax.shard_map(local, mesh=mesh, in_specs=in_specs, out_specs=out_specs, check_vma=False)
```

```python
import functools
import math

import jax
import jax.numpy as jnp
import numpy as np
from jax import lax
from jax.experimental import pallas as pl
from jax.experimental.pallas import tpu as pltpu
from jax.sharding import PartitionSpec as P

DFT_LEN = 256
GAP = 8
ANTENNA_BLOCK = 16
MERGED = 512
VMEM_LIMIT = 56 * 1024 * 1024


def shifted(value, axis, steps):
    count = lax.axis_size(axis)
    leading, last = (max(0, -steps), min(count, count - steps))
    return lax.ppermute(value, axis, [(source, source + steps) for source in range(leading, last)])


def dft_rows(frame_length, group_count):
    channels = frame_length // 2
    per_target = channels // group_count
    row = np.arange(frame_length)
    target = row // (2 * per_target)
    within = row % (2 * per_target)
    quadrature = within // per_target
    channel = target * per_target + within % per_target
    winding = np.arange(frame_length)[None, :] * channel[:, None] % frame_length
    angles = np.float32(2.0 * math.pi / frame_length) * winding.astype(np.float32)
    factor = np.float32(channels ** (-0.5))
    table = np.where(quadrature[:, None] == 0, np.cos(angles) * factor, -np.sin(angles) * factor)
    return jnp.asarray(table.astype(jnp.bfloat16))


def block_tables(length):
    half_len = length // 2
    factor = length ** (-0.5)
    sample = jnp.arange(length, dtype=jnp.int32)
    angles = (
        2.0 * math.pi / length * (sample[:, None] * sample[None, :] % length).astype(jnp.float32)
    )
    cosine_table = (jnp.cos(angles) * factor).astype(jnp.bfloat16)
    sine_table = (jnp.sin(angles) * factor).astype(jnp.bfloat16)
    forward_real = jnp.concatenate([cosine_table, -sine_table], axis=1)
    forward_imag = jnp.concatenate([sine_table, cosine_table], axis=1)
    back_cos = cosine_table[:, half_len:]
    back_sin = sine_table[:, half_len:]
    inverse_real = jnp.concatenate([back_cos, back_sin], axis=1)
    inverse_imag = jnp.concatenate([-back_sin, back_cos], axis=1)
    return (forward_real, forward_imag, inverse_real, inverse_imag)


def chirp_factor(delays, channel_count, channels, length):
    frequency = jnp.arange(length, dtype=jnp.int32)
    signed = jnp.where(frequency < length // 2, frequency, frequency - length).astype(jnp.float32)
    channel = jnp.arange(channel_count, dtype=jnp.int32).astype(jnp.float32)
    strength = (1.0 + channel / channels) ** (-3.0)
    sweep = signed * signed / (length * length)
    phases = (math.pi * delays.astype(jnp.float32))[None, :, None] * strength[
        :, None, None
    ] * sweep[None, None, :] - 0.5 * math.pi * frequency.astype(jnp.float32)[None, None, :]
    return (jnp.cos(phases), jnp.sin(phases))


def channelise_kernel(taps, frame, spectra, edge, *refs):
    taps_ref, table_ref, past_ref, now_ref = refs[:4]
    out_ref, w_ref, x_ref = refs[-3:]
    rows = now_ref.shape[0]
    past_frames = past_ref.shape[1] // frame
    group = 8
    lanes = 128
    at_edge = pl.program_id(0) == 0

    def filter_group(frames, first, lane):
        weights = [
            jnp.broadcast_to(taps_ref[k : k + 1, lane : lane + lanes], (8, lanes))
            for k in range(taps)
        ]
        for half in range(rows // 8):
            part = [f[half * 8 : half * 8 + 8] for f in frames]
            for i in range(group):
                total = weights[0] * part[i]
                for k in range(1, taps):
                    total = total + weights[k] * part[i + k]
                at = pl.multiple_of((first + i) * (rows + GAP) + half * 8, 8)
                w_ref[lane // lanes, pl.ds(at, 8), :] = total

    def earlier(start):
        value = past_ref[:, start : start + lanes]
        if edge:
            value = jnp.where(at_edge, refs[4][:, start : start + lanes], value)
        return value

    for lane in range(0, frame, lanes):
        frames = []
        for i in range(1 - taps, group):
            if i < 0:
                value = earlier((i + past_frames) * frame + lane)
            else:
                value = now_ref[:, i * frame + lane : i * frame + lane + lanes]
            frames.append(value.astype(jnp.float32))
        filter_group(frames, 0, lane)

    def later(step, carry):
        for lane in range(0, frame, lanes):
            frames = []
            for i in range(1 - taps, group):
                start = pl.multiple_of((step * group + i) * frame + lane, lanes)
                frames.append(now_ref[:, pl.ds(start, lanes)].astype(jnp.float32))
            filter_group(frames, step * group, lane)
        return carry

    lax.fori_loop(1, spectra // group, later, 0)

    def transform(pair, carry):
        parts = []
        for i in range(2):
            row = [
                w_ref[lane, pl.ds(pair * 2 + i, spectra, stride=rows + GAP), :].astype(jnp.bfloat16)
                for lane in range(frame // lanes)
            ]
            parts.append(jnp.concatenate(row, axis=1))
        both = jnp.concatenate(parts, axis=0)
        result = lax.dot_general(
            table_ref[...], both, (((1,), (1,)), ((), ())), preferred_element_type=jnp.float32
        )
        for i in range(2):
            at = pl.multiple_of((pair * 2 + i) * (frame + GAP), GAP)
            x_ref[pl.ds(at, frame), :] = result[:, i * spectra : (i + 1) * spectra]
        return carry

    lax.fori_loop(0, rows // 2, transform, 0, unroll=4)

    def arrange(step, carry):
        for i in range(8):
            j = step * 8 + i
            out_ref[j] = x_ref[pl.ds(j, rows, stride=frame + GAP), :].astype(jnp.bfloat16)
        return carry

    lax.fori_loop(0, frame // 8, arrange, 0)


def channelise(voltages, halo, filter_taps, table, first, count, spectra, low, high):
    taps, frame = filter_taps.shape
    rows = ANTENNA_BLOCK
    past_frames = halo.shape[1] // frame
    per_block = spectra // past_frames
    base = low // rows
    edge = first == 0
    operands = [filter_taps, table, voltages, voltages]
    specs = [
        pl.BlockSpec((taps, frame), lambda t, a: (0, 0)),
        pl.BlockSpec((frame, frame), lambda t, a: (0, 0)),
        pl.BlockSpec(
            (rows, past_frames * frame),
            lambda t, a: (base + a, jnp.maximum((first + t) * per_block - 1, 0)),
        ),
        pl.BlockSpec((rows, spectra * frame), lambda t, a: (base + a, first + t)),
    ]
    if edge:
        operands.append(halo)
        specs.append(pl.BlockSpec((rows, past_frames * frame), lambda t, a: (base + a, 0)))
    return pl.pallas_call(
        functools.partial(channelise_kernel, taps, frame, spectra, edge),
        grid=(count, (high - low) // rows),
        in_specs=specs,
        out_specs=pl.BlockSpec((frame, rows, spectra), lambda t, a: (0, a, t)),
        out_shape=jax.ShapeDtypeStruct((frame, high - low, count * spectra), jnp.bfloat16),
        scratch_shapes=[
            pltpu.VMEM((frame // 128, (spectra + 1) * (rows + GAP), 128), jnp.float32),
            pltpu.VMEM(((rows + 1) * (frame + GAP), spectra), jnp.float32),
        ],
        compiler_params=pltpu.CompilerParams(vmem_limit_bytes=VMEM_LIMIT),
        cost_estimate=pl.CostEstimate(
            flops=4 * count * (high - low) * spectra * frame * frame,
            bytes_accessed=4 * count * (high - low) * spectra * frame,
            transcendentals=0,
        ),
        name="channelise",
    )(*operands)


def beamform_kernel(cuts, weights_ref, *refs):
    out_ref = refs[-1]
    inputs = refs[:-1]
    groups = out_ref.shape[0]
    spectra = out_ref.shape[-1]
    beams = weights_ref.shape[2]

    def rows_of(quadrature):
        parts = []
        for ref in inputs[quadrature::2]:
            bounds = [0] + (cuts if len(inputs) == 2 else []) + [ref.shape[2]]
            for low, high in zip(bounds[:-1], bounds[1:]):
                parts.append(ref[:, 0, low:high, :].reshape(groups * (high - low), spectra))
        return parts[0] if len(parts) == 1 else jnp.concatenate(parts, axis=0)

    both = jnp.concatenate([rows_of(0), rows_of(1)], axis=1)
    share = beams // groups
    step = max(share, 128)
    for first in range(0, beams, step):
        by_real = jnp.dot(
            weights_ref[0, 0, first : first + step], both, preferred_element_type=jnp.float32
        )
        by_imag = jnp.dot(
            weights_ref[0, 1, first : first + step], both, preferred_element_type=jnp.float32
        )
        beam_real = (by_real[:, :spectra] - by_imag[:, spectra:]).astype(jnp.bfloat16)
        beam_imag = (by_real[:, spectra:] + by_imag[:, :spectra]).astype(jnp.bfloat16)
        low = first // share
        high = low + step // share
        out_ref[low:high, 0, 0] = beam_real.reshape(step // share, share, spectra)
        out_ref[low:high, 0, 1] = beam_imag.reshape(step // share, share, spectra)


def beamform(weights, received, cuts, first, count, spectra, low, high):
    per_target, _, beams, antennas = weights.shape
    groups = received[0].shape[0]
    share = beams // groups
    specs = [pl.BlockSpec((1, 2, beams, antennas), lambda c, t: (low + c, 0, 0, 0))]
    operands = [weights]
    for array in received:
        block = (groups, 1, array.shape[2], spectra)
        specs.append(pl.BlockSpec(block, lambda c, t: (0, low + c, 0, first + t)))
        specs.append(pl.BlockSpec(block, lambda c, t: (0, per_target + low + c, 0, first + t)))
        operands += [array, array]
    return pl.pallas_call(
        functools.partial(beamform_kernel, cuts),
        grid=(high - low, count),
        in_specs=specs,
        out_specs=pl.BlockSpec((groups, 1, 2, share, spectra), lambda c, t: (0, c, 0, 0, t)),
        out_shape=jax.ShapeDtypeStruct(
            (groups, high - low, 2, share, count * spectra), jnp.bfloat16
        ),
        compiler_params=pltpu.CompilerParams(vmem_limit_bytes=VMEM_LIMIT),
        cost_estimate=pl.CostEstimate(
            flops=8 * (high - low) * beams * antennas * spectra * count,
            bytes_accessed=4 * (high - low) * beams * (antennas + 2 * spectra * count),
            transcendentals=0,
        ),
        name="beamform",
    )(*operands)


def dedisperse_kernel(count, *refs):
    pieces = refs[: count + 1]
    cos_ref, sin_ref, fr_ref, fi_ref, ir_ref, ii_ref = refs[count + 1 : count + 7]
    out_ref = refs[-1]
    sources, chans, _, beams, advance = pieces[0].shape
    length = 2 * advance
    merged = sources * chans * beams
    chirp_real = cos_ref[...].reshape(merged, length)
    chirp_imag = sin_ref[...].reshape(merged, length)

    def part(ref, quadrature):
        return ref[:, :, quadrature].reshape(merged, advance)

    for m in range(count):
        before, after = pieces[m], pieces[m + 1]
        real = jnp.concatenate([part(before, 0), part(after, 0)], axis=1)
        imag = jnp.concatenate([part(before, 1), part(after, 1)], axis=1)
        spectrum = jnp.dot(real, fr_ref[...], preferred_element_type=jnp.float32) + jnp.dot(
            imag, fi_ref[...], preferred_element_type=jnp.float32
        )
        spec_real = spectrum[:, :length]
        spec_imag = spectrum[:, length:]
        filtered_real = (spec_real * chirp_real - spec_imag * chirp_imag).astype(jnp.bfloat16)
        filtered_imag = (spec_real * chirp_imag + spec_imag * chirp_real).astype(jnp.bfloat16)
        result = jnp.dot(filtered_real, ir_ref[...], preferred_element_type=jnp.float32) + jnp.dot(
            filtered_imag, ii_ref[...], preferred_element_type=jnp.float32
        )
        at = slice(m * advance, (m + 1) * advance)
        out_ref[:, :, 0, :, at] = result[:, :advance].reshape(sources, chans, beams, advance)
        out_ref[:, :, 1, :, at] = result[:, advance:].reshape(sources, chans, beams, advance)


def dedisperse(pieces, first, blocks, low, high, chans, chirp, tables, output):
    count = len(pieces) - 1
    groups, per_target, beams, length = chirp[0].shape
    advance = length // 2
    sources = max(1, min(groups, MERGED // (beams * chans)))

    def piece_spec(block, start):
        skip = (low - start) // chans
        return pl.BlockSpec(
            (sources, chans, 2, beams, advance), lambda g, c: (g, skip + c, 0, 0, block)
        )

    base = low // chans
    factor = pl.BlockSpec((sources, chans, beams, length), lambda g, c: (g, base + c, 0, 0))
    specs = [piece_spec(block, start) for _, block, start in pieces] + [factor] * 2
    specs += [pl.BlockSpec(t.shape, lambda g, c: (0, 0)) for t in tables]
    operands = [array for array, _, _ in pieces] + list(chirp) + list(tables)
    aliases = {}
    if output is not None:
        aliases = {len(operands): 0}
        operands.append(output)
        specs.append(pl.BlockSpec(memory_space=pl.ANY))
    return pl.pallas_call(
        functools.partial(dedisperse_kernel, count),
        grid=(groups // sources, (high - low) // chans),
        in_specs=specs,
        out_specs=pl.BlockSpec(
            (sources, chans, 2, beams, count * advance),
            lambda g, c: (g, base + c, 0, 0, first // count),
        ),
        out_shape=jax.ShapeDtypeStruct(
            (groups, per_target, 2, beams, blocks * advance), jnp.float32
        ),
        input_output_aliases=aliases,
        compiler_params=pltpu.CompilerParams(vmem_limit_bytes=VMEM_LIMIT),
        cost_estimate=pl.CostEstimate(
            flops=12 * count * groups * (high - low) * beams * length * length,
            bytes_accessed=groups * (high - low) * beams * advance * (12 * count + 20),
            transcendentals=0,
        ),
        name="dedisperse",
    )(*operands)


def local(voltages, filter_taps, beam_weights, antenna_of_row, beam_delay):
    group_count = lax.axis_size("grp")
    antenna_rows, samples = voltages.shape
    taps, frame = filter_taps.shape
    spectra = samples // frame
    channels = frame // 2
    antennas = antenna_of_row.shape[0]
    per_target = channels // group_count
    advance = DFT_LEN // 2
    blocks = spectra // advance
    last = blocks - 1

    table = dft_rows(frame, group_count)
    past_frames = -(-(taps - 1) // 8) * 8
    halo = shifted(voltages[:, samples - past_frames * frame :], "section", 1)

    cut = ANTENNA_BLOCK
    cuts = [cut] if cut < antenna_rows else []
    bounds = [0] + cuts + [antenna_rows]
    row_order = np.concatenate(
        [
            (np.arange(group_count)[:, None] * antenna_rows + np.arange(low, high)[None, :]).ravel()
            for low, high in zip(bounds[:-1], bounds[1:])
        ]
    )
    chosen = (
        jnp.arange(antennas, dtype=jnp.int32)[:, None] == antenna_of_row[row_order][None, :]
    ).astype(jnp.bfloat16)
    ordered = jnp.einsum(
        "ckba,ar->ckbr", beam_weights, chosen, preferred_element_type=jnp.float32
    ).astype(jnp.bfloat16)
    tables = block_tables(DFT_LEN)
    chirp = chirp_factor(beam_delay, channels, channels, DFT_LEN)
    chirp = tuple(c.reshape((group_count, per_target) + c.shape[1:]) for c in chirp)

    previous = None

    def exchange(value, previous):
        if previous is not None:
            value, previous = lax.optimization_barrier((value, previous))
        return lax.all_to_all(value, "grp", split_axis=0, concat_axis=0, tiled=True)

    def send_spectra(first, count, low, high, previous):
        value = channelise(voltages, halo, filter_taps, table, first, count, advance, low, high)
        value = value.reshape(group_count, 2 * per_target, high - low, count * advance)
        return exchange(value, previous)

    received_last = []
    for low, high in zip(bounds[:-1], bounds[1:]):
        previous = send_spectra(last, 1, low, high, previous)
        received_last.append(previous)
    received_rest = previous = send_spectra(0, last, 0, antenna_rows, previous)

    form = functools.partial(beamform, ordered)
    whole = (0, per_target)
    value = form(received_last, cuts, 0, 1, advance, *whole)
    value, chirp = lax.optimization_barrier((value, chirp))
    series_last = previous = exchange(value, previous)
    leading = shifted(series_last, "section", 1)

    tail = max(1, per_target // 8)
    middle = per_target - tail
    value = form([received_rest], cuts, 0, last, advance, 0, middle)
    series_head = previous = exchange(value, previous)
    value = form([received_rest], cuts, 0, last, advance, middle, per_target)
    value, leading = lax.optimization_barrier((value, leading))
    series_tail = exchange(value, previous)

    output = None
    for low, high, series in ((0, middle, series_head), (middle, per_target, series_tail)):
        pieces = [(leading, 0, 0)] + [(series, m, low) for m in range(last)] + [(series_last, 0, 0)]
        output = dedisperse(pieces, 0, blocks, low, high, tail, chirp, tables, output)
    return output.reshape((channels,) + output.shape[2:])


def solution(mesh):
    in_specs = (P("grp", "section"), P(), P("grp", None, None, None), P(), P("grp"))
    out_specs = P(None, None, "grp", "section")
    return jax.shard_map(local, mesh=mesh, in_specs=in_specs, out_specs=out_specs, check_vma=False)
```

```python
import functools
import math

import jax
import jax.numpy as jnp
import numpy as np
from jax import lax
from jax.experimental import pallas as pl
from jax.experimental.pallas import tpu as pltpu
from jax.sharding import PartitionSpec as P

DFT_LEN = 256
GAP = 8
ANTENNA_BLOCK = 16
MERGED = 1024
VMEM_LIMIT = 56 * 1024 * 1024


def shifted(value, axis, steps):
    count = lax.axis_size(axis)
    leading, last = (max(0, -steps), min(count, count - steps))
    return lax.ppermute(value, axis, [(source, source + steps) for source in range(leading, last)])


def dft_rows(frame_length, group_count):
    channels = frame_length // 2
    per_target = channels // group_count
    row = np.arange(frame_length)
    target = row // (2 * per_target)
    within = row % (2 * per_target)
    quadrature = within // per_target
    channel = target * per_target + within % per_target
    winding = np.arange(frame_length)[None, :] * channel[:, None] % frame_length
    angles = np.float32(2.0 * math.pi / frame_length) * winding.astype(np.float32)
    factor = np.float32(channels ** (-0.5))
    table = np.where(quadrature[:, None] == 0, np.cos(angles) * factor, -np.sin(angles) * factor)
    return jnp.asarray(table.astype(jnp.bfloat16))


def block_tables(length):
    half_len = length // 2
    factor = np.float32(length ** (-0.5))
    sample = np.arange(length)
    winding = (sample[:, None] * sample[None, :] % length).astype(np.float32)
    angles = np.float32(2.0 * math.pi / length) * winding
    cosine_table = np.cos(angles) * factor
    sine_table = np.sin(angles) * factor
    forward = np.block([[cosine_table, -sine_table], [sine_table, cosine_table]])
    back_cos = cosine_table[:, half_len:]
    back_sin = sine_table[:, half_len:]
    inverse = np.block([[back_cos, back_sin], [-back_sin, back_cos]])
    return (jnp.asarray(forward.astype(jnp.bfloat16)), jnp.asarray(inverse.astype(jnp.bfloat16)))


def chirp_factor(delays, channel_count, channels, length):
    frequency = jnp.arange(length, dtype=jnp.int32)
    signed = jnp.where(frequency < length // 2, frequency, frequency - length).astype(jnp.float32)
    channel = jnp.arange(channel_count, dtype=jnp.int32).astype(jnp.float32)
    strength = (1.0 + channel / channels) ** (-3.0)
    sweep = signed * signed / (length * length)
    phases = (math.pi * delays.astype(jnp.float32))[None, :, None] * strength[
        :, None, None
    ] * sweep[None, None, :] - 0.5 * math.pi * frequency.astype(jnp.float32)[None, None, :]
    return (jnp.cos(phases), jnp.sin(phases))


def channelise_kernel(taps, frame, spectra, edge, *refs):
    taps_ref, table_ref, past_ref, now_ref = refs[:4]
    out_ref, w_ref, x_ref = refs[-3:]
    rows = now_ref.shape[0]
    past_frames = past_ref.shape[1] // frame
    group = 8
    lanes = 128
    at_edge = pl.program_id(0) == 0

    def filter_group(frames, first, lane):
        weights = [
            jnp.broadcast_to(taps_ref[k : k + 1, lane : lane + lanes], (8, lanes))
            for k in range(taps)
        ]
        for half in range(rows // 8):
            part = [f[half * 8 : half * 8 + 8] for f in frames]
            for i in range(group):
                total = weights[0] * part[i]
                for k in range(1, taps):
                    total = total + weights[k] * part[i + k]
                at = pl.multiple_of((first + i) * (rows + GAP) + half * 8, 8)
                w_ref[lane // lanes, pl.ds(at, 8), :] = total

    def earlier(start):
        value = past_ref[:, start : start + lanes]
        if edge:
            value = jnp.where(at_edge, refs[4][:, start : start + lanes], value)
        return value

    for lane in range(0, frame, lanes):
        frames = []
        for i in range(1 - taps, group):
            if i < 0:
                value = earlier((i + past_frames) * frame + lane)
            else:
                value = now_ref[:, i * frame + lane : i * frame + lane + lanes]
            frames.append(value.astype(jnp.float32))
        filter_group(frames, 0, lane)

    def later(step, carry):
        for lane in range(0, frame, lanes):
            frames = []
            for i in range(1 - taps, group):
                start = pl.multiple_of((step * group + i) * frame + lane, lanes)
                frames.append(now_ref[:, pl.ds(start, lanes)].astype(jnp.float32))
            filter_group(frames, step * group, lane)
        return carry

    lax.fori_loop(1, spectra // group, later, 0)

    def transform(pair, carry):
        parts = []
        for i in range(2):
            row = [
                w_ref[lane, pl.ds(pair * 2 + i, spectra, stride=rows + GAP), :].astype(jnp.bfloat16)
                for lane in range(frame // lanes)
            ]
            parts.append(jnp.concatenate(row, axis=1))
        both = jnp.concatenate(parts, axis=0)
        result = lax.dot_general(
            table_ref[...], both, (((1,), (1,)), ((), ())), preferred_element_type=jnp.float32
        )
        for i in range(2):
            at = pl.multiple_of((pair * 2 + i) * (frame + GAP), GAP)
            x_ref[pl.ds(at, frame), :] = result[:, i * spectra : (i + 1) * spectra]
        return carry

    lax.fori_loop(0, rows // 2, transform, 0, unroll=8)

    def arrange(step, carry):
        for i in range(8):
            j = step * 8 + i
            out_ref[j] = x_ref[pl.ds(j, rows, stride=frame + GAP), :].astype(jnp.bfloat16)
        return carry

    lax.fori_loop(0, frame // 8, arrange, 0, unroll=4)


def channelise(voltages, halo, filter_taps, table, first, count, spectra, low, high):
    taps, frame = filter_taps.shape
    rows = ANTENNA_BLOCK
    past_frames = halo.shape[1] // frame
    per_block = spectra // past_frames
    base = low // rows
    edge = first == 0
    operands = [filter_taps, table, voltages, voltages]
    specs = [
        pl.BlockSpec((taps, frame), lambda t, a: (0, 0)),
        pl.BlockSpec((frame, frame), lambda t, a: (0, 0)),
        pl.BlockSpec(
            (rows, past_frames * frame),
            lambda t, a: (base + a, jnp.maximum((first + t) * per_block - 1, 0)),
        ),
        pl.BlockSpec((rows, spectra * frame), lambda t, a: (base + a, first + t)),
    ]
    if edge:
        operands.append(halo)
        specs.append(pl.BlockSpec((rows, past_frames * frame), lambda t, a: (base + a, 0)))
    return pl.pallas_call(
        functools.partial(channelise_kernel, taps, frame, spectra, edge),
        grid=(count, (high - low) // rows),
        in_specs=specs,
        out_specs=pl.BlockSpec((frame, rows, spectra), lambda t, a: (0, a, t)),
        out_shape=jax.ShapeDtypeStruct((frame, high - low, count * spectra), jnp.bfloat16),
        scratch_shapes=[
            pltpu.VMEM((frame // 128, (spectra + 1) * (rows + GAP), 128), jnp.float32),
            pltpu.VMEM(((rows + 1) * (frame + GAP), spectra), jnp.float32),
        ],
        compiler_params=pltpu.CompilerParams(vmem_limit_bytes=VMEM_LIMIT),
        cost_estimate=pl.CostEstimate(
            flops=4 * count * (high - low) * spectra * frame * frame,
            bytes_accessed=4 * count * (high - low) * spectra * frame,
            transcendentals=0,
        ),
        name="channelise",
    )(*operands)


def beamform_kernel(cuts, weights_ref, *refs):
    out_ref = refs[-1]
    inputs = refs[:-1]
    groups = out_ref.shape[0]
    spectra = out_ref.shape[-1]
    beams = weights_ref.shape[2]

    def rows_of(quadrature):
        parts = []
        for ref in inputs[quadrature::2]:
            bounds = [0] + (cuts if len(inputs) == 2 else []) + [ref.shape[2]]
            for low, high in zip(bounds[:-1], bounds[1:]):
                parts.append(ref[:, 0, low:high, :].reshape(groups * (high - low), spectra))
        return parts[0] if len(parts) == 1 else jnp.concatenate(parts, axis=0)

    both = jnp.concatenate([rows_of(0), rows_of(1)], axis=1)
    share = beams // groups
    step = max(share, 128)
    for first in range(0, beams, step):
        by_real = jnp.dot(
            weights_ref[0, 0, first : first + step], both, preferred_element_type=jnp.float32
        )
        by_imag = jnp.dot(
            weights_ref[0, 1, first : first + step], both, preferred_element_type=jnp.float32
        )
        beam_real = (by_real[:, :spectra] - by_imag[:, spectra:]).astype(jnp.bfloat16)
        beam_imag = (by_real[:, spectra:] + by_imag[:, :spectra]).astype(jnp.bfloat16)
        low = first // share
        high = low + step // share
        out_ref[low:high, 0, 0] = beam_real.reshape(step // share, share, spectra)
        out_ref[low:high, 0, 1] = beam_imag.reshape(step // share, share, spectra)


def beamform(weights, received, cuts, first, count, spectra, low, high):
    per_target, _, beams, antennas = weights.shape
    groups = received[0].shape[0]
    share = beams // groups
    specs = [pl.BlockSpec((1, 2, beams, antennas), lambda c, t: (low + c, 0, 0, 0))]
    operands = [weights]
    for array in received:
        block = (groups, 1, array.shape[2], spectra)
        specs.append(pl.BlockSpec(block, lambda c, t: (0, low + c, 0, first + t)))
        specs.append(pl.BlockSpec(block, lambda c, t: (0, per_target + low + c, 0, first + t)))
        operands += [array, array]
    return pl.pallas_call(
        functools.partial(beamform_kernel, cuts),
        grid=(high - low, count),
        in_specs=specs,
        out_specs=pl.BlockSpec((groups, 1, 2, share, spectra), lambda c, t: (0, c, 0, 0, t)),
        out_shape=jax.ShapeDtypeStruct(
            (groups, high - low, 2, share, count * spectra), jnp.bfloat16
        ),
        compiler_params=pltpu.CompilerParams(vmem_limit_bytes=VMEM_LIMIT),
        cost_estimate=pl.CostEstimate(
            flops=8 * (high - low) * beams * antennas * spectra * count,
            bytes_accessed=4 * (high - low) * beams * (antennas + 2 * spectra * count),
            transcendentals=0,
        ),
        name="beamform",
    )(*operands)


def dedisperse_kernel(count, *refs):
    pieces = refs[: count + 1]
    cos_ref, sin_ref, forward_ref, inverse_ref = refs[count + 1 : count + 5]
    out_ref = refs[-1]
    sources, chans, _, beams, advance = pieces[0].shape
    length = 2 * advance
    merged = sources * chans * beams
    chirp_real = cos_ref[...].reshape(merged, length)
    chirp_imag = sin_ref[...].reshape(merged, length)

    def part(ref, quadrature):
        return ref[:, :, quadrature].reshape(merged, advance)

    for m in range(count):
        before, after = pieces[m], pieces[m + 1]
        real = jnp.concatenate([part(before, 0), part(after, 0)], axis=1)
        imag = jnp.concatenate([part(before, 1), part(after, 1)], axis=1)
        spectrum = jnp.dot(real, forward_ref[:length], preferred_element_type=jnp.float32) + jnp.dot(
            imag, forward_ref[length:], preferred_element_type=jnp.float32
        )
        spec_real = spectrum[:, :length]
        spec_imag = spectrum[:, length:]
        filtered_real = (spec_real * chirp_real - spec_imag * chirp_imag).astype(jnp.bfloat16)
        filtered_imag = (spec_real * chirp_imag + spec_imag * chirp_real).astype(jnp.bfloat16)
        result = jnp.dot(
            filtered_real, inverse_ref[:length], preferred_element_type=jnp.float32
        ) + jnp.dot(filtered_imag, inverse_ref[length:], preferred_element_type=jnp.float32)
        at = slice(m * advance, (m + 1) * advance)
        out_ref[:, :, 0, :, at] = result[:, :advance].reshape(sources, chans, beams, advance)
        out_ref[:, :, 1, :, at] = result[:, advance:].reshape(sources, chans, beams, advance)


def dedisperse(pieces, first, blocks, low, high, chans, chirp, tables, output):
    count = len(pieces) - 1
    groups, per_target, beams, length = chirp[0].shape
    advance = length // 2
    merged = MERGED if high - low > chans else MERGED // 2
    sources = max(1, min(groups, merged // (beams * chans)))

    def piece_spec(block, start):
        skip = (low - start) // chans
        return pl.BlockSpec(
            (sources, chans, 2, beams, advance), lambda g, c: (g, skip + c, 0, 0, block)
        )

    base = low // chans
    factor = pl.BlockSpec((sources, chans, beams, length), lambda g, c: (g, base + c, 0, 0))
    specs = [piece_spec(block, start) for _, block, start in pieces] + [factor] * 2
    specs += [pl.BlockSpec(t.shape, lambda g, c: (0, 0)) for t in tables]
    operands = [array for array, _, _ in pieces] + list(chirp) + list(tables)
    aliases = {}
    if output is not None:
        aliases = {len(operands): 0}
        operands.append(output)
        specs.append(pl.BlockSpec(memory_space=pl.ANY))
    return pl.pallas_call(
        functools.partial(dedisperse_kernel, count),
        grid=(groups // sources, (high - low) // chans),
        in_specs=specs,
        out_specs=pl.BlockSpec(
            (sources, chans, 2, beams, count * advance),
            lambda g, c: (g, base + c, 0, 0, first // count),
        ),
        out_shape=jax.ShapeDtypeStruct(
            (groups, per_target, 2, beams, blocks * advance), jnp.float32
        ),
        input_output_aliases=aliases,
        compiler_params=pltpu.CompilerParams(vmem_limit_bytes=VMEM_LIMIT),
        cost_estimate=pl.CostEstimate(
            flops=12 * count * groups * (high - low) * beams * length * length,
            bytes_accessed=groups * (high - low) * beams * advance * (12 * count + 20),
            transcendentals=0,
        ),
        name="dedisperse",
    )(*operands)


def local(voltages, filter_taps, beam_weights, antenna_of_row, beam_delay):
    group_count = lax.axis_size("grp")
    antenna_rows, samples = voltages.shape
    taps, frame = filter_taps.shape
    spectra = samples // frame
    channels = frame // 2
    antennas = antenna_of_row.shape[0]
    per_target = channels // group_count
    advance = DFT_LEN // 2
    blocks = spectra // advance
    last = blocks - 1

    table = dft_rows(frame, group_count)
    past_frames = -(-(taps - 1) // 8) * 8
    halo = shifted(voltages[:, samples - past_frames * frame :], "section", 1)

    cut = ANTENNA_BLOCK
    cuts = [cut] if cut < antenna_rows else []
    bounds = [0] + cuts + [antenna_rows]
    row_order = np.concatenate(
        [
            (np.arange(group_count)[:, None] * antenna_rows + np.arange(low, high)[None, :]).ravel()
            for low, high in zip(bounds[:-1], bounds[1:])
        ]
    )
    chosen = (
        jnp.arange(antennas, dtype=jnp.int32)[:, None] == antenna_of_row[row_order][None, :]
    ).astype(jnp.bfloat16)
    ordered = jnp.einsum(
        "ckba,ar->ckbr", beam_weights, chosen, preferred_element_type=jnp.float32
    ).astype(jnp.bfloat16)
    tables = block_tables(DFT_LEN)
    chirp = chirp_factor(beam_delay, channels, channels, DFT_LEN)
    chirp = tuple(c.reshape((group_count, per_target) + c.shape[1:]) for c in chirp)

    previous = None

    def exchange(value, previous):
        if previous is not None:
            value, previous = lax.optimization_barrier((value, previous))
        return lax.all_to_all(value, "grp", split_axis=0, concat_axis=0, tiled=True)

    def send_spectra(first, count, low, high, previous):
        value = channelise(voltages, halo, filter_taps, table, first, count, advance, low, high)
        value = value.reshape(group_count, 2 * per_target, high - low, count * advance)
        return exchange(value, previous)

    received_last = []
    for low, high in zip(bounds[:-1], bounds[1:]):
        previous = send_spectra(last, 1, low, high, previous)
        received_last.append(previous)
    received_rest = previous = send_spectra(0, last, 0, antenna_rows, previous)

    form = functools.partial(beamform, ordered)
    whole = (0, per_target)
    value = form(received_last, cuts, 0, 1, advance, *whole)
    value, chirp = lax.optimization_barrier((value, chirp))
    series_last = previous = exchange(value, previous)
    leading = shifted(series_last, "section", 1)

    tail = max(1, per_target // 8)
    middle = per_target - tail
    value = form([received_rest], cuts, 0, last, advance, 0, middle)
    series_head = previous = exchange(value, previous)
    value = form([received_rest], cuts, 0, last, advance, middle, per_target)
    value, leading = lax.optimization_barrier((value, leading))
    series_tail = exchange(value, previous)

    output = None
    for low, high, series in ((0, middle, series_head), (middle, per_target, series_tail)):
        pieces = [(leading, 0, 0)] + [(series, m, low) for m in range(last)] + [(series_last, 0, 0)]
        output = dedisperse(pieces, 0, blocks, low, high, tail, chirp, tables, output)
    return output.reshape((channels,) + output.shape[2:])


def solution(mesh):
    in_specs = (P("grp", "section"), P(), P("grp", None, None, None), P(), P("grp"))
    out_specs = P(None, None, "grp", "section")
    return jax.shard_map(local, mesh=mesh, in_specs=in_specs, out_specs=out_specs, check_vma=False)
```

```python
import functools
import math

import jax
import jax.numpy as jnp
import numpy as np
from jax import lax
from jax.experimental import pallas as pl
from jax.experimental.pallas import tpu as pltpu
from jax.sharding import PartitionSpec as P

DFT_LEN = 256
GAP = 8
ANTENNA_BLOCK = 16
MERGED = 1024
VMEM_LIMIT = 56 * 1024 * 1024
SMALL_VMEM_LIMIT = 28 * 1024 * 1024


def shifted(value, axis, steps):
    count = lax.axis_size(axis)
    leading, last = (max(0, -steps), min(count, count - steps))
    return lax.ppermute(value, axis, [(source, source + steps) for source in range(leading, last)])


def dft_rows(frame_length, group_count):
    channels = frame_length // 2
    per_target = channels // group_count
    row = np.arange(frame_length)
    target = row // (2 * per_target)
    within = row % (2 * per_target)
    quadrature = within // per_target
    channel = target * per_target + within % per_target
    winding = np.arange(frame_length)[None, :] * channel[:, None] % frame_length
    angles = np.float32(2.0 * math.pi / frame_length) * winding.astype(np.float32)
    factor = np.float32(channels ** (-0.5))
    table = np.where(quadrature[:, None] == 0, np.cos(angles) * factor, -np.sin(angles) * factor)
    return jnp.asarray(table.astype(jnp.bfloat16))


def block_tables(length):
    half_len = length // 2
    factor = np.float32(length ** (-0.5))
    sample = np.arange(length)
    winding = (sample[:, None] * sample[None, :] % length).astype(np.float32)
    angles = np.float32(2.0 * math.pi / length) * winding
    cosine_table = np.cos(angles) * factor
    sine_table = np.sin(angles) * factor
    forward = np.block([[cosine_table, -sine_table], [sine_table, cosine_table]])
    back_cos = cosine_table[:, half_len:]
    back_sin = sine_table[:, half_len:]
    inverse = np.block([[back_cos, back_sin], [-back_sin, back_cos]])
    return (jnp.asarray(forward.astype(jnp.bfloat16)), jnp.asarray(inverse.astype(jnp.bfloat16)))


def chirp_factor(delays, channel_count, channels, length):
    frequency = jnp.arange(length, dtype=jnp.int32)
    signed = jnp.where(frequency < length // 2, frequency, frequency - length).astype(jnp.float32)
    channel = jnp.arange(channel_count, dtype=jnp.int32).astype(jnp.float32)
    strength = (1.0 + channel / channels) ** (-3.0)
    sweep = signed * signed / (length * length)
    phases = (math.pi * delays.astype(jnp.float32))[None, :, None] * strength[
        :, None, None
    ] * sweep[None, None, :] - 0.5 * math.pi * frequency.astype(jnp.float32)[None, None, :]
    return (jnp.cos(phases), jnp.sin(phases))


def channelise_kernel(taps, frame, spectra, edge, *refs):
    taps_ref, table_ref, past_ref, now_ref = refs[:4]
    out_ref, w_ref, x_ref = refs[-3:]
    rows = now_ref.shape[0]
    past_frames = past_ref.shape[1] // frame
    group = 8
    lanes = 128
    at_edge = pl.program_id(0) == 0

    def filter_group(frames, first, lane):
        weights = [
            jnp.broadcast_to(taps_ref[k : k + 1, lane : lane + lanes], (8, lanes))
            for k in range(taps)
        ]
        for half in range(rows // 8):
            part = [f[half * 8 : half * 8 + 8] for f in frames]
            for i in range(group):
                total = weights[0] * part[i]
                for k in range(1, taps):
                    total = total + weights[k] * part[i + k]
                at = pl.multiple_of((first + i) * (rows + GAP) + half * 8, 8)
                w_ref[lane // lanes, pl.ds(at, 8), :] = total

    def earlier(start):
        value = past_ref[:, start : start + lanes]
        if edge:
            value = jnp.where(at_edge, refs[4][:, start : start + lanes], value)
        return value

    for lane in range(0, frame, lanes):
        frames = []
        for i in range(1 - taps, group):
            if i < 0:
                value = earlier((i + past_frames) * frame + lane)
            else:
                value = now_ref[:, i * frame + lane : i * frame + lane + lanes]
            frames.append(value.astype(jnp.float32))
        filter_group(frames, 0, lane)

    def later(step, carry):
        for lane in range(0, frame, lanes):
            frames = []
            for i in range(1 - taps, group):
                start = pl.multiple_of((step * group + i) * frame + lane, lanes)
                frames.append(now_ref[:, pl.ds(start, lanes)].astype(jnp.float32))
            filter_group(frames, step * group, lane)
        return carry

    lax.fori_loop(1, spectra // group, later, 0)

    def transform(pair, carry):
        parts = []
        for i in range(2):
            row = [
                w_ref[lane, pl.ds(pair * 2 + i, spectra, stride=rows + GAP), :].astype(jnp.bfloat16)
                for lane in range(frame // lanes)
            ]
            parts.append(jnp.concatenate(row, axis=1))
        both = jnp.concatenate(parts, axis=0)
        result = lax.dot_general(
            table_ref[...], both, (((1,), (1,)), ((), ())), preferred_element_type=jnp.float32
        )
        for i in range(2):
            at = pl.multiple_of((pair * 2 + i) * (frame + GAP), GAP)
            x_ref[pl.ds(at, frame), :] = result[:, i * spectra : (i + 1) * spectra]
        return carry

    lax.fori_loop(0, rows // 2, transform, 0, unroll=8)

    def arrange(step, carry):
        for i in range(8):
            j = step * 8 + i
            out_ref[j] = x_ref[pl.ds(j, rows, stride=frame + GAP), :].astype(jnp.bfloat16)
        return carry

    lax.fori_loop(0, frame // 8, arrange, 0, unroll=4)


def channelise(voltages, halo, filter_taps, table, first, count, spectra, low, high):
    taps, frame = filter_taps.shape
    rows = ANTENNA_BLOCK
    past_frames = halo.shape[1] // frame
    per_block = spectra // past_frames
    base = low // rows
    edge = first == 0
    operands = [filter_taps, table, voltages, voltages]
    specs = [
        pl.BlockSpec((taps, frame), lambda t, a: (0, 0)),
        pl.BlockSpec((frame, frame), lambda t, a: (0, 0)),
        pl.BlockSpec(
            (rows, past_frames * frame),
            lambda t, a: (base + a, jnp.maximum((first + t) * per_block - 1, 0)),
        ),
        pl.BlockSpec((rows, spectra * frame), lambda t, a: (base + a, first + t)),
    ]
    if edge:
        operands.append(halo)
        specs.append(pl.BlockSpec((rows, past_frames * frame), lambda t, a: (base + a, 0)))
    return pl.pallas_call(
        functools.partial(channelise_kernel, taps, frame, spectra, edge),
        grid=(count, (high - low) // rows),
        in_specs=specs,
        out_specs=pl.BlockSpec((frame, rows, spectra), lambda t, a: (0, a, t)),
        out_shape=jax.ShapeDtypeStruct((frame, high - low, count * spectra), jnp.bfloat16),
        scratch_shapes=[
            pltpu.VMEM((frame // 128, (spectra + 1) * (rows + GAP), 128), jnp.float32),
            pltpu.VMEM(((rows + 1) * (frame + GAP), spectra), jnp.float32),
        ],
        compiler_params=pltpu.CompilerParams(vmem_limit_bytes=VMEM_LIMIT),
        cost_estimate=pl.CostEstimate(
            flops=4 * count * (high - low) * spectra * frame * frame,
            bytes_accessed=4 * count * (high - low) * spectra * frame,
            transcendentals=0,
        ),
        name="channelise",
    )(*operands)


def beamform_kernel(cuts, weights_ref, *refs):
    out_ref = refs[-1]
    inputs = refs[:-1]
    groups = out_ref.shape[0]
    spectra = out_ref.shape[-1]
    beams = weights_ref.shape[2]

    def rows_of(quadrature):
        parts = []
        for ref in inputs[quadrature::2]:
            bounds = [0] + (cuts if len(inputs) == 2 else []) + [ref.shape[2]]
            for low, high in zip(bounds[:-1], bounds[1:]):
                parts.append(ref[:, 0, low:high, :].reshape(groups * (high - low), spectra))
        return parts[0] if len(parts) == 1 else jnp.concatenate(parts, axis=0)

    both = jnp.concatenate([rows_of(0), rows_of(1)], axis=1)
    share = beams // groups
    step = max(share, 128)
    for first in range(0, beams, step):
        by_real = jnp.dot(
            weights_ref[0, 0, first : first + step], both, preferred_element_type=jnp.float32
        )
        by_imag = jnp.dot(
            weights_ref[0, 1, first : first + step], both, preferred_element_type=jnp.float32
        )
        beam_real = (by_real[:, :spectra] - by_imag[:, spectra:]).astype(jnp.bfloat16)
        beam_imag = (by_real[:, spectra:] + by_imag[:, :spectra]).astype(jnp.bfloat16)
        low = first // share
        high = low + step // share
        out_ref[low:high, 0, 0] = beam_real.reshape(step // share, share, spectra)
        out_ref[low:high, 0, 1] = beam_imag.reshape(step // share, share, spectra)


def beamform(weights, received, cuts, first, count, spectra, low, high):
    per_target, _, beams, antennas = weights.shape
    groups = received[0].shape[0]
    share = beams // groups
    specs = [pl.BlockSpec((1, 2, beams, antennas), lambda c, t: (low + c, 0, 0, 0))]
    operands = [weights]
    for array in received:
        block = (groups, 1, array.shape[2], spectra)
        specs.append(pl.BlockSpec(block, lambda c, t: (0, low + c, 0, first + t)))
        specs.append(pl.BlockSpec(block, lambda c, t: (0, per_target + low + c, 0, first + t)))
        operands += [array, array]
    return pl.pallas_call(
        functools.partial(beamform_kernel, cuts),
        grid=(high - low, count),
        in_specs=specs,
        out_specs=pl.BlockSpec((groups, 1, 2, share, spectra), lambda c, t: (0, c, 0, 0, t)),
        out_shape=jax.ShapeDtypeStruct(
            (groups, high - low, 2, share, count * spectra), jnp.bfloat16
        ),
        compiler_params=pltpu.CompilerParams(vmem_limit_bytes=VMEM_LIMIT),
        cost_estimate=pl.CostEstimate(
            flops=8 * (high - low) * beams * antennas * spectra * count,
            bytes_accessed=4 * (high - low) * beams * (antennas + 2 * spectra * count),
            transcendentals=0,
        ),
        name="beamform",
    )(*operands)


def dedisperse_kernel(count, *refs):
    pieces = refs[: count + 1]
    cos_ref, sin_ref, forward_ref, inverse_ref = refs[count + 1 : count + 5]
    out_ref = refs[-1]
    sources, chans, _, beams, advance = pieces[0].shape
    length = 2 * advance
    merged = sources * chans * beams
    chirp_real = cos_ref[...].reshape(merged, length)
    chirp_imag = sin_ref[...].reshape(merged, length)

    def part(ref, quadrature):
        return ref[:, :, quadrature].reshape(merged, advance)

    for m in range(count):
        before, after = pieces[m], pieces[m + 1]
        real = jnp.concatenate([part(before, 0), part(after, 0)], axis=1)
        imag = jnp.concatenate([part(before, 1), part(after, 1)], axis=1)
        spectrum = jnp.dot(real, forward_ref[:length], preferred_element_type=jnp.float32) + jnp.dot(
            imag, forward_ref[length:], preferred_element_type=jnp.float32
        )
        spec_real = spectrum[:, :length]
        spec_imag = spectrum[:, length:]
        filtered_real = (spec_real * chirp_real - spec_imag * chirp_imag).astype(jnp.bfloat16)
        filtered_imag = (spec_real * chirp_imag + spec_imag * chirp_real).astype(jnp.bfloat16)
        result = jnp.dot(
            filtered_real, inverse_ref[:length], preferred_element_type=jnp.float32
        ) + jnp.dot(filtered_imag, inverse_ref[length:], preferred_element_type=jnp.float32)
        at = slice(m * advance, (m + 1) * advance)
        out_ref[:, :, 0, :, at] = result[:, :advance].reshape(sources, chans, beams, advance)
        out_ref[:, :, 1, :, at] = result[:, advance:].reshape(sources, chans, beams, advance)


def dedisperse(pieces, first, blocks, low, high, chans, chirp, tables, output):
    count = len(pieces) - 1
    groups, per_target, beams, length = chirp[0].shape
    advance = length // 2
    large = high - low > chans
    merged = MERGED if large else MERGED // 2
    sources = max(1, min(groups, merged // (beams * chans)))

    def piece_spec(block, start):
        skip = (low - start) // chans
        return pl.BlockSpec(
            (sources, chans, 2, beams, advance), lambda g, c: (g, skip + c, 0, 0, block)
        )

    base = low // chans
    factor = pl.BlockSpec((sources, chans, beams, length), lambda g, c: (g, base + c, 0, 0))
    specs = [piece_spec(block, start) for _, block, start in pieces] + [factor] * 2
    specs += [pl.BlockSpec(t.shape, lambda g, c: (0, 0)) for t in tables]
    operands = [array for array, _, _ in pieces] + list(chirp) + list(tables)
    aliases = {}
    if output is not None:
        aliases = {len(operands): 0}
        operands.append(output)
        specs.append(pl.BlockSpec(memory_space=pl.ANY))
    return pl.pallas_call(
        functools.partial(dedisperse_kernel, count),
        grid=(groups // sources, (high - low) // chans),
        in_specs=specs,
        out_specs=pl.BlockSpec(
            (sources, chans, 2, beams, count * advance),
            lambda g, c: (g, base + c, 0, 0, first // count),
        ),
        out_shape=jax.ShapeDtypeStruct(
            (groups, per_target, 2, beams, blocks * advance), jnp.float32
        ),
        input_output_aliases=aliases,
        compiler_params=pltpu.CompilerParams(
            vmem_limit_bytes=VMEM_LIMIT if large else SMALL_VMEM_LIMIT
        ),
        cost_estimate=pl.CostEstimate(
            flops=12 * count * groups * (high - low) * beams * length * length,
            bytes_accessed=groups * (high - low) * beams * advance * (12 * count + 20),
            transcendentals=0,
        ),
        name="dedisperse",
    )(*operands)


def local(voltages, filter_taps, beam_weights, antenna_of_row, beam_delay):
    group_count = lax.axis_size("grp")
    antenna_rows, samples = voltages.shape
    taps, frame = filter_taps.shape
    spectra = samples // frame
    channels = frame // 2
    antennas = antenna_of_row.shape[0]
    per_target = channels // group_count
    advance = DFT_LEN // 2
    blocks = spectra // advance
    last = blocks - 1

    table = dft_rows(frame, group_count)
    past_frames = -(-(taps - 1) // 8) * 8
    halo = shifted(voltages[:, samples - past_frames * frame :], "section", 1)

    cut = ANTENNA_BLOCK
    cuts = [cut] if cut < antenna_rows else []
    bounds = [0] + cuts + [antenna_rows]
    row_order = np.concatenate(
        [
            (np.arange(group_count)[:, None] * antenna_rows + np.arange(low, high)[None, :]).ravel()
            for low, high in zip(bounds[:-1], bounds[1:])
        ]
    )
    chosen = (
        jnp.arange(antennas, dtype=jnp.int32)[:, None] == antenna_of_row[row_order][None, :]
    ).astype(jnp.bfloat16)
    ordered = jnp.einsum(
        "ckba,ar->ckbr", beam_weights, chosen, preferred_element_type=jnp.float32
    ).astype(jnp.bfloat16)
    tables = block_tables(DFT_LEN)
    chirp = chirp_factor(beam_delay, channels, channels, DFT_LEN)
    chirp = tuple(c.reshape((group_count, per_target) + c.shape[1:]) for c in chirp)

    previous = None

    def exchange(value, previous):
        if previous is not None:
            value, previous = lax.optimization_barrier((value, previous))
        return lax.all_to_all(value, "grp", split_axis=0, concat_axis=0, tiled=True)

    def send_spectra(first, count, low, high, previous):
        value = channelise(voltages, halo, filter_taps, table, first, count, advance, low, high)
        value = value.reshape(group_count, 2 * per_target, high - low, count * advance)
        return exchange(value, previous)

    received_last = []
    for low, high in zip(bounds[:-1], bounds[1:]):
        previous = send_spectra(last, 1, low, high, previous)
        received_last.append(previous)
    received_rest = previous = send_spectra(0, last, 0, antenna_rows, previous)

    form = functools.partial(beamform, ordered)
    whole = (0, per_target)
    value = form(received_last, cuts, 0, 1, advance, *whole)
    value, chirp = lax.optimization_barrier((value, chirp))
    series_last = previous = exchange(value, previous)
    leading = shifted(series_last, "section", 1)

    tail = max(1, per_target // 8)
    middle = per_target - tail
    value = form([received_rest], cuts, 0, last, advance, 0, middle)
    series_head = previous = exchange(value, previous)
    value = form([received_rest], cuts, 0, last, advance, middle, per_target)
    value, leading = lax.optimization_barrier((value, leading))
    series_tail = exchange(value, previous)

    output = None
    for low, high, series in ((0, middle, series_head), (middle, per_target, series_tail)):
        pieces = [(leading, 0, 0)] + [(series, m, low) for m in range(last)] + [(series_last, 0, 0)]
        output = dedisperse(pieces, 0, blocks, low, high, tail, chirp, tables, output)
    return output.reshape((channels,) + output.shape[2:])


def solution(mesh):
    in_specs = (P("grp", "section"), P(), P("grp", None, None, None), P(), P("grp"))
    out_specs = P(None, None, "grp", "section")
    return jax.shard_map(local, mesh=mesh, in_specs=in_specs, out_specs=out_specs, check_vma=False)
```
